256 devices in a mesh: row: 16 (over y, x), col: 16 (over z, core).
Axes of the slice: x: 4, y: 4, z: 8, core: 2. Of those that a mesh axis runs over, the one named last changes fastest.
Arguments:
- matrix: bfloat16 [24576, 24576], P('row', 'col'), may hold values from -6 to 6
- inverses: bfloat16 [2, 256, 256], replicated, may hold values from -0.09 to 0.1, as said below
Outputs:
- factored: bfloat16 [24576, 24576], P('row', 'col')
- panels: bfloat16 [24576, 512], P('row')
The draws below stay inside these ranges and needn't reach their ends.
Inputs may be any that keep to these rules, and one draw needn't show every extreme that they name: `inverses`: each of the two matrices is lower triangular with a diagonal between 0.05 and 0.1.
All inputs are finite; a program needn't handle non-finite values.
Results may differ from the reference program's by a relative error of at most 0.0057.
Values may be sent and summed in bfloat16 or wider, within the bound.
No kernel may reach another device: no remote copies, remote signals or barrier semaphores. Data moves between devices by JAX's collectives and lax.ppermute only.
A program may use at most 128 MiB of HBM per device.

```python
import jax
import jax.numpy as jnp
from jax import lax

NB = 256
BLK_ROW = 6
BLK_COL = 6
NBLK = 96
ORDER = 24576
N_ROW = 16
N_COL = 16


def draw_inverses(key, part):
    key_strict, key_diagonal = jax.random.split(jax.random.fold_in(key, 7))
    strict = jnp.clip(jax.random.normal(key_strict, (2, NB, NB), jnp.float32) / 64.0, -0.09, 0.09)
    diagonal = jax.random.uniform(key_diagonal, (2, NB), jnp.float32, 0.05, 0.0995)
    row_index = lax.broadcasted_iota(jnp.int32, (2, NB, NB), 1)
    col_index = lax.broadcasted_iota(jnp.int32, (2, NB, NB), 2)
    lower_part = jnp.where(row_index > col_index, strict, 0.0)
    return (lower_part + jnp.where(row_index == col_index, diagonal[:, :, None], 0.0)).astype(jnp.bfloat16)


def block_levels(rng, dims, cuts, least, largest):
    loudness = 1.0
    for position, blocks in cuts:
        steps = jax.random.uniform(jax.random.fold_in(jax.random.fold_in(rng, 6), position), (blocks,), jnp.float32, least / len(cuts), largest / len(cuts))
        loudness = loudness * jnp.repeat(jnp.exp(steps), dims[position] // blocks).reshape((-1,) + (1,) * (len(dims) - 1 - position))
    return loudness


def centred(key, dims, spread, reach, cuts=(), kind=jnp.bfloat16):
    values = spread * jax.random.normal(key, dims, jnp.float32)
    if cuts:
        values = values * block_levels(key, dims, cuts, -0.22, 0.18)
    return jnp.clip(values, -reach, reach).astype(kind)


def setup_inputs(seed: int = 0) -> dict:
    arg_keys = jax.random.split(jax.random.key(seed), 3)
    matrix = centred(arg_keys[0], (ORDER, ORDER), 1.0, 6.0, ((0, 16), (1, 16)))
    inverses = draw_inverses(jax.random.fold_in(arg_keys[2], 71), 0)
    return {"matrix": matrix, "inverses": inverses}


def reference(matrix, inverses):
    stored = jnp.arange(NBLK, dtype=jnp.int32)
    row_global = (stored % BLK_ROW) * N_ROW + stored // BLK_ROW
    col_global = (stored % BLK_COL) * N_COL + stored // BLK_COL
    col_source = (col_global % N_ROW) * BLK_ROW + col_global // N_ROW
    row_of = jnp.repeat(row_global, NB)

    def factor(panel, inverse, start_block):
        product = jnp.dot(panel, inverse.T, preferred_element_type=jnp.float32)
        return jnp.where((row_of >= start_block)[:, None], product, jnp.zeros_like(product)).astype(jnp.bfloat16)

    def transposed(left_rows):
        return left_rows.reshape(NBLK, NB, NB)[col_source].reshape(ORDER, NB)

    first_factor = factor(matrix[:, :NB], inverses[0], 1)
    first_cols = transposed(first_factor)
    head_block = first_cols[BLK_COL * NB:BLK_COL * NB + NB]
    head = (matrix[:, BLK_COL * NB:BLK_COL * NB + NB].astype(jnp.float32)
            - jnp.dot(first_factor, head_block.T, preferred_element_type=jnp.float32)).astype(jnp.bfloat16)
    second_factor = factor(head, inverses[1], 2)
    second_cols = transposed(second_factor)

    blocks = matrix.reshape(NBLK, NB, ORDER)
    first_blocks = first_factor.reshape(NBLK, NB, NB)
    second_blocks = second_factor.reshape(NBLK, NB, NB)
    first_trans = first_cols.T
    second_trans = second_cols.T

    def one_block(pieces):
        block_rows, first_rows, second_rows = pieces
        value = block_rows.astype(jnp.float32)
        value = value - jnp.dot(first_rows, first_trans, preferred_element_type=jnp.float32)
        value = value - jnp.dot(second_rows, second_trans, preferred_element_type=jnp.float32)
        return value.astype(jnp.bfloat16)

    factored = lax.map(one_block, (blocks, first_blocks, second_blocks)).reshape(ORDER, ORDER)
    return factored, jnp.concatenate([first_factor, second_factor], axis=1)
```

```python
import functools

import jax
import jax.numpy as jnp
from jax import lax
from jax.experimental import pallas as pl
from jax.experimental.pallas import tpu as pltpu
from jax.sharding import PartitionSpec as P

BOTH = ("row", "col")
NB = 256
SLOTS = 6
LINE = 8
CUT = NB // LINE


def dot_t(left, right):
    return lax.dot_general(
        left, right, (((1,), (1,)), ((), ())), preferred_element_type=jnp.float32
    )


def finish_kernel(where_ref, matrix, inverses, own, near1, near2, near3, far,
                  swap1, swap2, swap3, swap4, cols, factored, panels,
                  held, inv, rows_x, cols_x, head_g, rows_f, cols_f, result,
                  sem_m, sem_x, sem_o):
    row, col = where_ref[0], where_ref[1]
    z, core = col // 2, lax.rem(col, 2)
    copies = []

    def start(src, dst, sem):
        copy = pltpu.make_async_copy(src, dst, sem)
        copy.start()
        return copy

    early = [start(inverses, inv, sem_x.at[0])]
    for h in range(2):
        for s in range(LINE):
            early.append(start(cols.at[2 * s + h], cols_x.at[h, :, s], sem_x.at[0]))

    def place(msg, slot):
        for h in range(2):
            copies.append(start(msg.at[pl.ds(SLOTS * h, SLOTS)], rows_x.at[h, :, slot], sem_x.at[1]))
        copies.append(start(msg.at[2 * SLOTS], head_g.at[slot], sem_x.at[1]))

    place(own, z)
    for d, (near, swap) in enumerate(((near1, swap1), (near2, swap2), (near3, swap3)), 1):
        up, down = lax.rem(z + d, LINE), lax.rem(z + LINE - d, LINE)
        place(near, jnp.where(core == 0, up, down))
        place(swap, jnp.where(core == 0, down, up))
    across = lax.rem(z + LINE // 2, LINE)
    copies.append(start(far.at[pl.ds(0, SLOTS)], rows_x.at[core, :, across], sem_x.at[1]))
    copies.append(start(swap4.at[pl.ds(0, SLOTS)], rows_x.at[1 - core, :, across], sem_x.at[1]))
    copies.append(start(far.at[SLOTS], head_g.at[across], sem_x.at[1]))
    loads = [start(matrix.at[pl.ds(NB * b, NB)], held.at[b], sem_m.at[b]) for b in range(SLOTS)]

    for c in early + copies:
        c.wait()
    lower0, lower1 = inv[0], inv[1]
    pivot = dot_t(head_g[...].reshape(NB, NB), lower0).astype(jnp.bfloat16)

    def factor(x, f, rank):
        for b in range(SLOTS):
            block = b * 16 + rank
            at = pl.ds(NB * b, NB)
            first = dot_t(x[0, b].reshape(NB, NB), lower0)
            first = jnp.where(block >= 1, first, 0.0).astype(jnp.bfloat16)
            f[at, pl.ds(0, NB)] = first
            head = (x[1, b].reshape(NB, NB).astype(jnp.float32) - dot_t(first, pivot)).astype(jnp.bfloat16)
            second = dot_t(head, lower1)
            f[at, pl.ds(NB, NB)] = jnp.where(block >= 2, second, 0.0).astype(jnp.bfloat16)

    factor(rows_x, rows_f, row)
    stores = [start(rows_f, panels, sem_o.at[SLOTS])]
    factor(cols_x, cols_f, col)
    for b in range(SLOTS):
        loads[b].wait()
        at = pl.ds(NB * b, NB)
        value = held[b].astype(jnp.float32) - dot_t(rows_f[at, :], cols_f[...])
        result[b] = value.astype(jnp.bfloat16)
        stores.append(start(result.at[b], factored.at[at], sem_o.at[b]))
    for c in stores:
        c.wait()


def finish(place, matrix, inverses, *pieces):
    any_space = pl.BlockSpec(memory_space=pl.ANY)
    rows, columns = matrix.shape
    return pl.pallas_call(
        finish_kernel,
        out_shape=(
            jax.ShapeDtypeStruct(matrix.shape, jnp.bfloat16),
            jax.ShapeDtypeStruct((rows, 2 * NB), jnp.bfloat16),
        ),
        in_specs=[pl.BlockSpec(memory_space=pltpu.SMEM)] + [any_space] * (2 + len(pieces)),
        out_specs=(any_space, any_space),
        scratch_shapes=[
            pltpu.VMEM((SLOTS, NB, columns), jnp.bfloat16),
            pltpu.VMEM((2, NB, NB), jnp.bfloat16),
            pltpu.VMEM((2, SLOTS, LINE, CUT, NB), jnp.bfloat16),
            pltpu.VMEM((2, SLOTS, LINE, CUT, NB), jnp.bfloat16),
            pltpu.VMEM((LINE, CUT, NB), jnp.bfloat16),
            pltpu.VMEM((rows, 2 * NB), jnp.bfloat16),
            pltpu.VMEM((columns, 2 * NB), jnp.bfloat16),
            pltpu.VMEM((SLOTS, NB, columns), jnp.bfloat16),
            pltpu.SemaphoreType.DMA((SLOTS,)),
            pltpu.SemaphoreType.DMA((2,)),
            pltpu.SemaphoreType.DMA((SLOTS + 1,)),
        ],
        compiler_params=pltpu.CompilerParams(vmem_limit_bytes=40 * 1024 * 1024),
        cost_estimate=pl.CostEstimate(
            flops=2 * rows * columns * 2 * NB, bytes_accessed=4 * rows * columns, transcendentals=0
        ),
    )(place, matrix, inverses, *pieces)


def moves(step):
    pairs = []
    for row in range(16):
        for z in range(LINE):
            for core in range(2):
                to = step(row, z, core)
                if to is not None:
                    pairs.append((row * 16 + 2 * z + core, to[0] * 16 + 2 * (to[1] % LINE) + to[2]))
    return pairs


def send(value, pairs):
    return lax.ppermute(value, BOTH, pairs)


def shards(matrix, inverses):
    row, col = lax.axis_index("row"), lax.axis_index("col")
    z, core = col // 2, col % 2
    cut = matrix[:, :NB].reshape(SLOTS, LINE, CUT, NB)
    mine = jnp.where(z == 0, cut[:, 0], 0)
    for d in (1, 2, 3, 7, 6, 5, 4):
        mine = mine + send(cut[:, d], moves(lambda r, zz, h: (r, d, h) if zz == 0 else None))
    crossed = send(mine, [(r * 16 + c, c * 16 + r) for r in range(16) for c in range(16)])
    pivot = lax.all_to_all(jnp.broadcast_to(mine[:1], (16, CUT, NB)), "row", 0, 0, tiled=True)[1:2]
    theirs = send(jnp.concatenate([mine, pivot]), moves(lambda r, zz, h: (r, zz, 1 - h)))
    is0 = core == 0
    own = jnp.concatenate([
        jnp.where(is0, mine, theirs[:SLOTS]),
        jnp.where(is0, theirs[:SLOTS], mine),
        jnp.where(is0, pivot, theirs[SLOTS:]),
    ])
    near = [send(own, moves(lambda r, zz, h: (r, zz - d if h == 0 else zz + d, h))) for d in (1, 2, 3)]
    far = send(jnp.concatenate([mine, own[2 * SLOTS:]]), moves(lambda r, zz, h: (r, zz + 4, h)))
    cols = lax.all_to_all(jnp.broadcast_to(crossed[None], (16,) + crossed.shape), "row", 0, 0, tiled=True)
    swaps = [send(v, moves(lambda r, zz, h: (r, zz, 1 - h))) for v in (*near, far)]
    place = jnp.stack([row, col]).astype(jnp.int32)
    return finish(place, matrix, inverses, own, *near, far, *swaps, cols)


def solution(mesh):
    return jax.shard_map(
        shards,
        mesh=mesh,
        in_specs=(P("row", "col"), P()),
        out_specs=(P("row", "col"), P("row", None)),
        check_vma=False,
    )
```

```python
import jax
import jax.numpy as jnp
from jax import lax
from jax.experimental import pallas as pl
from jax.experimental.pallas import tpu as pltpu
from jax.sharding import PartitionSpec as P

BOTH = ("row", "col")
NB = 256
SLOTS = 6
SIDE = 16
LINE = 8
CUT = NB // LINE
PIECE = SLOTS * CUT

SMEM = pl.BlockSpec(memory_space=pltpu.SMEM)
VMEM = pl.BlockSpec(memory_space=pltpu.VMEM)
HBM = pl.BlockSpec(memory_space=pltpu.HBM)
ANY = pl.BlockSpec(memory_space=pl.ANY)
MIB = 1024 * 1024


def ring(a, b, n):
    return min((a - b) % n, (b - a) % n)


def targets():
    table = []
    for rank in range(SIDE):
        def depth(q):
            return ring(q // 2, rank // 2, LINE)

        def spread(k):
            return ring(k // 4, rank // 4, 4) + ring(k % 4, rank % 4, 4)

        pieces = sorted(range(SIDE), key=lambda q: (-depth(q), q))
        places = sorted(range(SIDE), key=lambda k: (spread(k), (k - rank) % SIDE))
        row = [0] * SIDE
        for q, k in zip(pieces, places):
            row[q] = k
        table.append(row)
    return table


TARGETS = targets()
LEFT, RIGHT = pl.ds(0, NB), pl.ds(NB, NB)


def dot_t(left, right):
    return lax.dot_general(
        left, right, (((1,), (1,)), ((), ())), preferred_element_type=jnp.float32
    )


def keep(f, columns, rank, least):
    @pl.when(rank < least)
    def _():
        f[pl.ds(0, NB), columns] = jnp.zeros((NB, NB), jnp.bfloat16)


def factor(f, raw0, raw1, pivot, inv, rank):
    f[:, LEFT] = dot_t(raw0, inv[0]).astype(jnp.bfloat16)
    keep(f, LEFT, rank, 1)
    head = (raw1.astype(jnp.float32) - dot_t(f[:, LEFT], pivot)).astype(jnp.bfloat16)
    f[:, RIGHT] = dot_t(head, inv[1]).astype(jnp.bfloat16)
    keep(f, RIGHT, rank, 2)


def finish_kernel(order_ref, inv, own, near1, near2, near3, swap1, swap2, swap3, far, swap4, cols, matrix,
                  factored, panels, held, edge, rows_x, cols_x, base, rows_f, cols_f, sem_m, sem_e, sem_o):
    row, col = lax.axis_index("row"), lax.axis_index("col")
    z, core = col // 2, lax.rem(col, 2)
    edges = [pltpu.make_async_copy(src, edge.at[i], sem_e.at[i]) for i, src in enumerate((far, swap4))]
    for c in edges:
        c.start()
    loads = []
    for b in range(SLOTS):
        loads.append(pltpu.make_async_copy(matrix.at[pl.ds(NB * b, NB)], held.at[b], sem_m.at[b]))
        loads[b].start()

    def place(msg, slot):
        for h in range(2):
            rows_x[h, :, slot] = msg[pl.ds(PIECE * h, PIECE)].reshape(SLOTS, CUT, NB)
        base[slot] = msg[pl.ds(2 * PIECE, CUT)]

    place(own, z)
    for d, (near, swap) in enumerate(((near1, swap1), (near2, swap2), (near3, swap3)), 1):
        up, down = lax.rem(z + d, LINE), lax.rem(z + LINE - d, LINE)
        place(near, jnp.where(core == 0, up, down))
        place(swap, jnp.where(core == 0, down, up))
    for s in range(LINE):
        for h in range(2):
            cols_x[h, :, s] = cols[order_ref[col * SIDE + 2 * s + h]].reshape(SLOTS, CUT, NB)
    for c in edges:
        c.wait()
    across = lax.rem(z + LINE // 2, LINE)
    rows_x[core, :, across] = edge[0, pl.ds(0, PIECE)].reshape(SLOTS, CUT, NB)
    rows_x[1 - core, :, across] = edge[1, pl.ds(0, PIECE)].reshape(SLOTS, CUT, NB)
    base[across] = edge[0, pl.ds(PIECE, CUT)]
    pivot = dot_t(base[...].reshape(NB, NB), inv[0]).astype(jnp.bfloat16)
    factor(rows_f, rows_x[0].reshape(SLOTS * NB, NB), rows_x[1].reshape(SLOTS * NB, NB), pivot, inv, row)
    stores = [pltpu.make_async_copy(rows_f, panels, sem_o.at[SLOTS])]
    stores[0].start()
    factor(cols_f, cols_x[0].reshape(SLOTS * NB, NB), cols_x[1].reshape(SLOTS * NB, NB), pivot, inv, col)
    for b in range(SLOTS):
        loads[b].wait()
        at = pl.ds(NB * b, NB)
        value = held[b].astype(jnp.float32) - dot_t(rows_f[at, :], cols_f[...])
        held[b] = value.astype(jnp.bfloat16)
        stores.append(pltpu.make_async_copy(held.at[b], factored.at[at], sem_o.at[b]))
        stores[-1].start()
    for c in stores:
        c.wait()


def finish(inverses, own, near, swaps, far, cols, matrix):
    rows, columns = matrix.shape
    matrix = pltpu.with_memory_space_constraint(matrix, pltpu.HBM)
    return pl.pallas_call(
        finish_kernel,
        out_shape=(
            jax.ShapeDtypeStruct(matrix.shape, jnp.bfloat16),
            jax.ShapeDtypeStruct((rows, 2 * NB), jnp.bfloat16),
        ),
        in_specs=[SMEM] + [VMEM] * 8 + [ANY, ANY, VMEM, HBM],
        out_specs=(HBM, HBM),
        scratch_shapes=[
            pltpu.VMEM((SLOTS, NB, columns), jnp.bfloat16),
            pltpu.VMEM((2,) + far.shape, jnp.bfloat16),
            pltpu.VMEM((2, SLOTS, LINE, CUT, NB), jnp.bfloat16),
            pltpu.VMEM((2, SLOTS, LINE, CUT, NB), jnp.bfloat16),
            pltpu.VMEM((LINE, CUT, NB), jnp.bfloat16),
            pltpu.VMEM((rows, 2 * NB), jnp.bfloat16),
            pltpu.VMEM((columns, 2 * NB), jnp.bfloat16),
            pltpu.SemaphoreType.DMA((SLOTS,)),
            pltpu.SemaphoreType.DMA((2,)),
            pltpu.SemaphoreType.DMA((SLOTS + 1,)),
        ],
        compiler_params=pltpu.CompilerParams(vmem_limit_bytes=36 * MIB),
        cost_estimate=pl.CostEstimate(
            flops=2 * rows * columns * 2 * NB, bytes_accessed=4 * rows * columns, transcendentals=0
        ),
    )(jnp.asarray(TARGETS, jnp.int32).reshape(-1), inverses, own, *near, *swaps[:3], far, swaps[3], cols, matrix)


def moves(step):
    pairs = []
    for row in range(SIDE):
        for z in range(LINE):
            for core in range(2):
                to = step(row, z, core)
                if to is not None:
                    pairs.append((row * SIDE + 2 * z + core, to[0] * SIDE + 2 * (to[1] % LINE) + to[2]))
    return pairs


def send(value, pairs):
    return lax.ppermute(value, BOTH, pairs)


def shared(piece, axis, groups):
    copies = len(groups[0])
    spread = jnp.broadcast_to(piece[None], (copies,) + piece.shape).reshape(-1, NB)
    return lax.all_to_all(spread, axis, 0, 0, tiled=True, axis_index_groups=groups).reshape(
        (copies,) + piece.shape)


PLANE = [list(range(SIDE))]
LINES = [[2 * z + h for z in range(LINE)] for h in range(2)]


def shards(matrix, inverses):
    row, col = lax.axis_index("row"), lax.axis_index("col")
    z = col // 2
    cut = matrix[:, :NB].reshape(SLOTS, LINE, CUT, NB)
    mine = jnp.where(z == 0, cut[:, 0], 0)
    for d in (1, 5, 6, 7, 3, 2, 4):
        mine = mine + send(cut[:, d], moves(lambda r, zz, h: (r, d, h) if zz == 0 else None))
    mine = mine.reshape(PIECE, NB)
    crossed = send(mine, [(r * SIDE + q, TARGETS[r][q] * SIDE + r) for r in range(SIDE) for q in range(SIDE)])
    head = shared(mine[:CUT], "row", PLANE)[1]
    over = moves(lambda r, zz, h: (r, zz, 1 - h))
    theirs = send(jnp.concatenate([mine, head]), over)
    is0 = col % 2 == 0
    own = jnp.concatenate([
        jnp.where(is0, mine, theirs[:PIECE]),
        jnp.where(is0, theirs[:PIECE], mine),
        jnp.where(is0, head, theirs[PIECE:]),
    ])
    near = [send(own, moves(lambda r, zz, h: (r, zz - d if h == 0 else zz + d, h))) for d in (1, 2, 3)]
    far = send(jnp.concatenate([mine, own[2 * PIECE:]]), moves(lambda r, zz, h: (r, zz + LINE // 2, h)))
    cols = shared(crossed, "row", PLANE)
    swaps = [send(v, over) for v in (*near, far)]
    return finish(inverses, own, near, swaps, far, cols, matrix)


def solution(mesh):
    return jax.shard_map(
        shards,
        mesh=mesh,
        in_specs=(P("row", "col"), P()),
        out_specs=(P("row", "col"), P("row", None)),
        check_vma=False,
    )
```

```python
import jax
import jax.numpy as jnp
from jax import lax
from jax.experimental import pallas as pl
from jax.experimental.pallas import tpu as pltpu
from jax.sharding import PartitionSpec as P

BOTH = ("row", "col")
NB = 256
SLOTS = 6
SIDE = 16
LINE = 8
CUT = NB // LINE
PIECE = SLOTS * CUT
PARTS = 3
STRIP = SLOTS * NB // PARTS

VMEM = pl.BlockSpec(memory_space=pltpu.VMEM)
HBM = pl.BlockSpec(memory_space=pltpu.HBM)
ANY = pl.BlockSpec(memory_space=pl.ANY)
MIB = 1024 * 1024


def ring(a, b, n):
    return min((a - b) % n, (b - a) % n)


def targets():
    table = []
    for rank in range(SIDE):
        def depth(q):
            return ring(q // 2, rank // 2, LINE)

        def spread(k):
            return ring(k // 4, rank // 4, 4) + ring(k % 4, rank % 4, 4)

        pieces = sorted(range(SIDE), key=lambda q: (-depth(q), q))
        places = sorted(range(SIDE), key=lambda k: (spread(k), (k - rank) % SIDE))
        row = [0] * SIDE
        for q, k in zip(pieces, places):
            row[q] = k
        table.append(row)
    return table


TARGETS = targets()


def packed(numbers):
    word = sum(number << (4 * i) for i, number in enumerate(numbers))
    return word - (1 << 32) if word >= 1 << 31 else word


def target(q, rank):
    low = packed([TARGETS[r][q] for r in range(SIDE // 2)])
    high = packed([TARGETS[r][q] for r in range(SIDE // 2, SIDE)])
    word = jnp.where(rank < SIDE // 2, jnp.int32(low), jnp.int32(high))
    return jnp.bitwise_and(jnp.right_shift(word, 4 * lax.rem(rank, SIDE // 2)), 15)

LEFT, RIGHT = pl.ds(0, NB), pl.ds(NB, NB)


def dot_t(left, right):
    return lax.dot_general(
        left, right, (((1,), (1,)), ((), ())), preferred_element_type=jnp.float32
    )


def keep(f, columns, rank, least):
    @pl.when(rank < least)
    def _():
        f[pl.ds(0, NB), columns] = jnp.zeros((NB, NB), jnp.bfloat16)


def factor(f, raw0, raw1, pivot, inv, rank):
    f[:, LEFT] = dot_t(raw0, inv[0]).astype(jnp.bfloat16)
    keep(f, LEFT, rank, 1)
    head = (raw1.astype(jnp.float32) - dot_t(f[:, LEFT], pivot)).astype(jnp.bfloat16)
    f[:, RIGHT] = dot_t(head, inv[1]).astype(jnp.bfloat16)
    keep(f, RIGHT, rank, 2)


def finish_kernel(inv, own, near1, near2, near3, swap1, swap2, swap3, far, swap4, cols, matrix,
                  factored, panels, held, edge, rows_x, cols_x, base, rows_f, cols_f, sem_m, sem_e, sem_o):
    row, col = lax.axis_index("row"), lax.axis_index("col")
    z, core = col // 2, lax.rem(col, 2)
    edges = [pltpu.make_async_copy(src, edge.at[i], sem_e.at[i]) for i, src in enumerate((far, swap4))]
    for c in edges:
        c.start()
    loads = []
    for b in range(PARTS):
        at = pl.ds(STRIP * b, STRIP)
        loads.append(pltpu.make_async_copy(matrix.at[at], held.at[at], sem_m.at[b]))
        loads[b].start()

    def place(msg, slot):
        for h in range(2):
            rows_x[h, :, slot] = msg[pl.ds(PIECE * h, PIECE)].reshape(SLOTS, CUT, NB)
        base[slot] = msg[pl.ds(2 * PIECE, CUT)]

    place(own, z)
    for d, (near, swap) in enumerate(((near1, swap1), (near2, swap2), (near3, swap3)), 1):
        up, down = lax.rem(z + d, LINE), lax.rem(z + LINE - d, LINE)
        place(near, jnp.where(core == 0, up, down))
        place(swap, jnp.where(core == 0, down, up))
    for s in range(LINE):
        for h in range(2):
            cols_x[h, :, s] = cols[target(2 * s + h, col)].reshape(SLOTS, CUT, NB)
    for c in edges:
        c.wait()
    across = lax.rem(z + LINE // 2, LINE)
    rows_x[core, :, across] = edge[0, pl.ds(0, PIECE)].reshape(SLOTS, CUT, NB)
    rows_x[1 - core, :, across] = edge[1, pl.ds(0, PIECE)].reshape(SLOTS, CUT, NB)
    base[across] = edge[0, pl.ds(PIECE, CUT)]
    pivot = dot_t(base[...].reshape(NB, NB), inv[0]).astype(jnp.bfloat16)
    factor(rows_f, rows_x[0].reshape(SLOTS * NB, NB), rows_x[1].reshape(SLOTS * NB, NB), pivot, inv, row)
    stores = [pltpu.make_async_copy(rows_f, panels, sem_o.at[PARTS])]
    stores[0].start()
    factor(cols_f, cols_x[0].reshape(SLOTS * NB, NB), cols_x[1].reshape(SLOTS * NB, NB), pivot, inv, col)
    for b in range(PARTS):
        loads[b].wait()
        at = pl.ds(STRIP * b, STRIP)
        value = held[at, :].astype(jnp.float32) - dot_t(rows_f[at, :], cols_f[...])
        held[at, :] = value.astype(jnp.bfloat16)
        stores.append(pltpu.make_async_copy(held.at[at], factored.at[at], sem_o.at[b]))
        stores[-1].start()
    for c in stores:
        c.wait()


def finish(inverses, own, near, swaps, far, cols, matrix):
    rows, columns = matrix.shape
    matrix = pltpu.with_memory_space_constraint(matrix, pltpu.HBM)
    return pl.pallas_call(
        finish_kernel,
        out_shape=(
            jax.ShapeDtypeStruct(matrix.shape, jnp.bfloat16),
            jax.ShapeDtypeStruct((rows, 2 * NB), jnp.bfloat16),
        ),
        in_specs=[VMEM] * 8 + [ANY, ANY, VMEM, HBM],
        out_specs=(HBM, HBM),
        scratch_shapes=[
            pltpu.VMEM((rows, columns), jnp.bfloat16),
            pltpu.VMEM((2,) + far.shape, jnp.bfloat16),
            pltpu.VMEM((2, SLOTS, LINE, CUT, NB), jnp.bfloat16),
            pltpu.VMEM((2, SLOTS, LINE, CUT, NB), jnp.bfloat16),
            pltpu.VMEM((LINE, CUT, NB), jnp.bfloat16),
            pltpu.VMEM((rows, 2 * NB), jnp.bfloat16),
            pltpu.VMEM((columns, 2 * NB), jnp.bfloat16),
            pltpu.SemaphoreType.DMA((PARTS,)),
            pltpu.SemaphoreType.DMA((2,)),
            pltpu.SemaphoreType.DMA((PARTS + 1,)),
        ],
        compiler_params=pltpu.CompilerParams(vmem_limit_bytes=36 * MIB),
        cost_estimate=pl.CostEstimate(
            flops=2 * rows * columns * 2 * NB, bytes_accessed=4 * rows * columns, transcendentals=0
        ),
    )(inverses, own, *near, *swaps[:3], far, swaps[3], cols, matrix)


def moves(step):
    pairs = []
    for row in range(SIDE):
        for z in range(LINE):
            for core in range(2):
                to = step(row, z, core)
                if to is not None:
                    pairs.append((row * SIDE + 2 * z + core, to[0] * SIDE + 2 * (to[1] % LINE) + to[2]))
    return pairs


def send(value, pairs):
    return lax.ppermute(value, BOTH, pairs)


def shared(piece, axis, groups):
    copies = len(groups[0])
    spread = jnp.broadcast_to(piece[None], (copies,) + piece.shape).reshape(-1, NB)
    return lax.all_to_all(spread, axis, 0, 0, tiled=True, axis_index_groups=groups).reshape(
        (copies,) + piece.shape)


PLANE = [list(range(SIDE))]
LINES = [[2 * z + h for z in range(LINE)] for h in range(2)]


def shards(matrix, inverses):
    row, col = lax.axis_index("row"), lax.axis_index("col")
    z = col // 2
    cut = matrix[:, :NB].reshape(SLOTS, LINE, CUT, NB)
    mine = jnp.where(z == 0, cut[:, 0], 0)
    for d in (1, 5, 6, 7, 3, 2, 4):
        mine = mine + send(cut[:, d], moves(lambda r, zz, h: (r, d, h) if zz == 0 else None))
    mine = mine.reshape(PIECE, NB)
    crossed = send(mine, [(r * SIDE + q, TARGETS[r][q] * SIDE + r) for r in range(SIDE) for q in range(SIDE)])
    head = shared(mine[:CUT], "row", PLANE)[1]
    over = moves(lambda r, zz, h: (r, zz, 1 - h))
    theirs = send(jnp.concatenate([mine, head]), over)
    is0 = col % 2 == 0
    own = jnp.concatenate([
        jnp.where(is0, mine, theirs[:PIECE]),
        jnp.where(is0, theirs[:PIECE], mine),
        jnp.where(is0, head, theirs[PIECE:]),
    ])
    near = [send(own, moves(lambda r, zz, h: (r, zz - d if h == 0 else zz + d, h))) for d in (1, 2, 3)]
    far = send(jnp.concatenate([mine, own[2 * PIECE:]]), moves(lambda r, zz, h: (r, zz + LINE // 2, h)))
    cols = shared(crossed, "row", PLANE)
    swaps = [send(v, over) for v in (*near, far)]
    return finish(inverses, own, near, swaps, far, cols, matrix)


def solution(mesh):
    return jax.shard_map(
        shards,
        mesh=mesh,
        in_specs=(P("row", "col"), P()),
        out_specs=(P("row", "col"), P("row", None)),
        check_vma=False,
    )
```
